256 devices in a mesh: lon: 4 (over x), lat: 64 (over z, y, core).
Axes of the slice: x: 4, y: 4, z: 8, core: 2. Of those that a mesh axis runs over, the one named last changes fastest.
Arguments:
- tokens: bfloat16 [2, 384, 192, 512], P(None, 'lat', 'lon'), may hold values from -6 to 6
- qkv_weight: bfloat16 [512, 1536], replicated, may hold values from -0.25 to 0.25
- out_weight: bfloat16 [512, 512], replicated, may hold values from -0.25 to 0.25
- attn_gain: float32 [512], replicated, may hold values from 0.5 to 1.5
- logit_scale: float32 [8], replicated, may hold values from 4 to 16
- merge_weight: bfloat16 [2048, 1024], replicated, may hold values from -0.125 to 0.125
- merge_gain: float32 [2048], replicated, may hold values from 0.5 to 1.5
- split_weight: bfloat16 [1024, 2048], replicated, may hold values from -0.1875 to 0.1875
- split_gain: float32 [512], replicated, may hold values from 0.5 to 1.5
Outputs:
- decoded: bfloat16 [2, 384, 192, 512], P(None, 'lat', 'lon')
The draws below stay inside these ranges and needn't reach their ends.
All inputs are finite; a program needn't handle non-finite values.
Results may differ from the reference program's by a relative error of at most 0.015.
Values may be sent and summed in bfloat16 or wider, within the bound.
No kernel may reach another device: no remote copies, remote signals or barrier semaphores. Data moves between devices by JAX's collectives and lax.ppermute only.
A program may use at most 128 MiB of HBM per device.

```python
import math
import jax
import jax.numpy as jnp
from jax import lax

D = 512
DC = 1024
HEADS = 8
LEVELS = 2
NLAT = 384
NLON = 192


def steps_of(rng, dims, cuts, least, high):
    level = 1.0
    for axis_at, blocks in cuts:
        draws = jax.random.uniform(jax.random.fold_in(jax.random.fold_in(rng, 6), axis_at), (blocks,), jnp.float32, least / len(cuts), high / len(cuts))
        level = level * jnp.repeat(jnp.exp(draws), dims[axis_at] // blocks).reshape((-1,) + (1,) * (len(dims) - 1 - axis_at))
    return level


def scatter_about(own_key, shape, spread, most, split=(), dtype=jnp.bfloat16):
    result = spread * jax.random.normal(own_key, shape, jnp.float32)
    if split:
        result = result * steps_of(own_key, shape, split, -0.22, 0.18)
    return jnp.clip(result, -most, most).astype(dtype)


def setup_inputs(seed: int = 0) -> dict:
    streams_of = jax.random.split(jax.random.key(seed), 10)
    tokens = scatter_about(streams_of[0], (LEVELS, NLAT, NLON, D), 1.0, 6.0, ((1, 64), (2, 4)))
    qkv_weight = scatter_about(streams_of[1], (D, 3 * D), D ** -0.5, 0.25)
    out_weight = scatter_about(streams_of[2], (D, D), D ** -0.5, 0.25)
    attn_gain = jnp.clip(1.0 + 0.1 * jax.random.normal(streams_of[3], (D,), jnp.float32), 0.5, 1.5)
    logit_scale = jnp.clip(jnp.exp(jax.random.uniform(streams_of[4], (HEADS,), jnp.float32, math.log(4.0), math.log(16.0))), 4.0, 16.0)
    merge_weight = scatter_about(streams_of[5], (4 * D, DC), (4 * D) ** -0.5, 0.125)
    merge_gain = jnp.clip(1.0 + 0.1 * jax.random.normal(streams_of[6], (4 * D,), jnp.float32), 0.5, 1.5)
    split_weight = scatter_about(streams_of[7], (DC, 4 * D), DC ** -0.5, 0.1875)
    split_gain = jnp.clip(1.0 + 0.1 * jax.random.normal(streams_of[8], (D,), jnp.float32), 0.5, 1.5)
    return {"tokens": tokens, "qkv_weight": qkv_weight, "out_weight": out_weight, "attn_gain": attn_gain, "logit_scale": logit_scale, "merge_weight": merge_weight, "merge_gain": merge_gain, "split_weight": split_weight, "split_gain": split_gain}


def layer_norm(value, gain):
    value = value.astype(jnp.float32)
    centered = value - lax.optimization_barrier(jnp.mean(value, -1, keepdims=True))
    variance = lax.optimization_barrier(jnp.mean(centered * centered, -1, keepdims=True))
    return centered * lax.rsqrt(variance + 1e-05) * gain

def partition(array):
    depth, height, span, feats = array.shape
    shaped = array.reshape(depth // 2, 2, height // 6, 6, span // 12, 12, feats)
    shaped = shaped.transpose(0, 2, 4, 1, 3, 5, 6)
    return shaped.reshape(depth // 2 * (height // 6) * (span // 12), 144, feats)

def unpartition(array, depth, height, span):
    feats = array.shape[-1]
    shaped = array.reshape(depth // 2, height // 6, span // 12, 2, 6, 12, feats)
    shaped = shaped.transpose(0, 3, 1, 4, 2, 5, 6)
    return shaped.reshape(depth, height, span, feats)

def window_attention(query, keyval, valid, scales):
    depth, height, span, channel_width = query.shape
    head_count = scales.shape[0]
    window_size = channel_width // head_count
    qwin = partition(query).astype(jnp.float32)
    token_count = qwin.shape[0]
    qwin = qwin.reshape(token_count, 144, head_count, window_size)
    key_value_window = partition(keyval)
    kwin = key_value_window[:, :, :channel_width].astype(jnp.float32).reshape(token_count, 144, head_count, window_size)
    vwin = key_value_window[:, :, channel_width:].astype(jnp.float32).reshape(token_count, 144, head_count, window_size)
    mwin = partition(valid[:, :, :, None])[:, :, 0]
    qnorm = qwin * lax.rsqrt(lax.optimization_barrier(jnp.sum(qwin * qwin, -1, keepdims=True)) + 1e-06)
    knorm = kwin * lax.rsqrt(lax.optimization_barrier(jnp.sum(kwin * kwin, -1, keepdims=True)) + 1e-06)
    scores = jnp.einsum('wqhd,wkhd->whqk', qnorm, knorm, precision=lax.Precision.HIGHEST)
    scores = scores * scales[None, :, None, None]
    expo = jnp.exp(scores) * mwin[:, None, None, :]
    softmax_weight = (expo / lax.optimization_barrier(jnp.sum(expo, -1, keepdims=True))).astype(jnp.bfloat16)
    attended_output = jnp.einsum('nxtm,nmxv->ntxv', softmax_weight.astype(jnp.float32), vwin)
    attended_output = attended_output.astype(jnp.bfloat16).reshape(token_count, 144, channel_width)
    return unpartition(attended_output, depth, height, span)

def merge_split(skip, merge_weight, merge_gain, split_weight, split_gain):
    levels, rows, cols, channel_width = skip.shape
    blocks = skip.reshape(levels, rows // 2, 2, cols // 2, 2, channel_width).transpose(0, 1, 3, 4, 2, 5)
    merged = blocks.reshape(-1, 4 * channel_width)
    merged_normed = layer_norm(merged, merge_gain).astype(jnp.bfloat16)
    coarse = jnp.dot(merged_normed, merge_weight, preferred_element_type=jnp.float32).astype(jnp.bfloat16)
    expanded = jnp.dot(coarse, split_weight, preferred_element_type=jnp.float32)
    expanded = layer_norm(expanded.reshape(-1, 4, channel_width), split_gain)
    expanded = expanded.reshape(levels, rows // 2, cols // 2, 2, 2, channel_width).transpose(0, 1, 4, 2, 3, 5)
    expanded = expanded.reshape(levels, rows, cols, channel_width)
    return (skip.astype(jnp.float32) + expanded).astype(jnp.bfloat16)

def reference(tokens, qkv_weight, out_weight, attn_gain, logit_scale, merge_weight, merge_gain, split_weight, split_gain):
    levels, rows, cols, channel_width = tokens.shape
    normed = layer_norm(tokens, attn_gain).astype(jnp.bfloat16)
    flat = normed.reshape(-1, channel_width)
    query = jnp.dot(flat, qkv_weight[:, :channel_width], preferred_element_type=jnp.float32).astype(jnp.bfloat16)
    query = query.reshape(levels, rows, cols, channel_width)
    keyval = jnp.dot(flat, qkv_weight[:, channel_width:], preferred_element_type=jnp.float32).astype(jnp.bfloat16)
    keyval = keyval.reshape(levels, rows, cols, 2 * channel_width)
    valid = jnp.ones((levels, rows, cols), jnp.float32)
    columns = cols // 12

    def place(array):
        array = jnp.roll(array, 6, axis=2)
        padding = [(1, 1), (3, 3), (0, 0)] + [(0, 0)] * (array.ndim - 3)
        array = jnp.pad(array, padding)
        array = array.reshape(array.shape[:2] + (columns, 12) + array.shape[3:])
        return jnp.moveaxis(array, 2, 0)

    def one_column(item):
        return window_attention(item[0], item[1], item[2], logit_scale)
    attended_output = lax.map(one_column, (place(query), place(keyval), place(valid)))
    attended_output = jnp.moveaxis(attended_output, 0, 2).reshape(levels + 2, rows + 6, cols, channel_width)
    attended_output = jnp.roll(attended_output[1:-1, 3:-3], -6, axis=2)
    projected = jnp.dot(attended_output.reshape(-1, channel_width), out_weight, preferred_element_type=jnp.float32)
    skip = (tokens.astype(jnp.float32) + projected.reshape(levels, rows, cols, channel_width)).astype(jnp.bfloat16)
    return merge_split(skip, merge_weight, merge_gain, split_weight, split_gain)
```

```python
import jax
import jax.numpy as jnp
from jax import lax
from jax.experimental import pallas as pl
from jax.experimental.pallas import tpu as pltpu
from jax.sharding import PartitionSpec as P

BF = jnp.bfloat16
F32 = jnp.float32
D = 512
LOG2E = 1.4426950408889634
VMEM = pl.BlockSpec(memory_space=pltpu.VMEM)
PARAMS = pltpu.CompilerParams(vmem_limit_bytes=24 * 2**20)


def dot(a, b):
    return jnp.dot(a, b, preferred_element_type=F32)


def dot_t(a, b):
    return lax.dot_general(a, b, (((1,), (1,)), ((), ())), preferred_element_type=F32)


def layer_norm(value, gain):
    centered = value - jnp.mean(value, -1, keepdims=True)
    variance = jnp.mean(centered * centered, -1, keepdims=True)
    return centered * lax.rsqrt(variance + 1e-05) * gain


def head_scaled(value, block, extra):
    rounded = value.astype(BF)
    squares = rounded * rounded
    sums = jnp.concatenate([dot(squares[:, :256], block), dot(squares[:, 256:], block)], 1)
    return value * (lax.rsqrt(sums + 1e-06) * extra)


def stack_heads(q):
    lane = lax.broadcasted_iota(jnp.int32, q.shape, 1)
    return jnp.concatenate(
        [jnp.where((lane >= 64 * h) & (lane < 64 * h + 64), q, 0.0) for h in range(4)], 0
    ).astype(BF)


def unstack_heads(value, m, split):
    lane = lax.broadcasted_iota(jnp.int32, (m, 128), 1)
    halves = []
    for g in range(2):
        col = slice(128 * g, 128 * g + 128) if split else slice(0, 128)
        first = value[2 * g * m : (2 * g + 1) * m, col]
        second = value[(2 * g + 1) * m : (2 * g + 2) * m, col]
        halves.append(jnp.where(lane < 64, first, second))
    return jnp.concatenate(halves, 1)


def scores_to_sums(q, k, v, mask, ones, heads):
    m = q.shape[0]
    inverse = lax.rsqrt(dot_t(heads, k * k) + 1e-06)
    scores = dot_t(stack_heads(q), k)
    weight = [jnp.exp2(scores[m * h : m * h + m] * inverse[h : h + 1]) for h in range(4)]
    weight = jnp.concatenate(weight, 0).astype(BF) * mask
    return (
        unstack_heads(dot(weight, v), m, True),
        unstack_heads(dot(weight, ones), m, False),
    )


def head_rows():
    row = lax.broadcasted_iota(jnp.int32, (16, 256), 0)
    lane = lax.broadcasted_iota(jnp.int32, (16, 256), 1)
    return jnp.where(row == lax.shift_right_logical(lane, 6), 1.0, 0.0).astype(BF)


def window(col):
    return lax.shift_right_logical((col + 18) * 5462, 16)


def present_rows():
    lat = lax.axis_index("lat")
    return jnp.where((lat > 0) & (lat < lax.axis_size("lat") - 1), 1.0, 0.0)


def main_mask(ch, present):
    query = lax.broadcasted_iota(jnp.int32, (72, 192), 0)
    key = lax.broadcasted_iota(jnp.int32, (72, 192), 1)
    row = (query >= 24).astype(jnp.int32) + (query >= 48).astype(jnp.int32)
    same = window(24 * ch + query - 24 * row) == window(16 * ch + (key & 31))
    value = jnp.where(same, jnp.where(key < 96, 1.0, present), 0.0)
    return jnp.concatenate([value] * 4, 0).astype(BF)


def edge_mask(side, present):
    query = lax.broadcasted_iota(jnp.int32, (96, 192), 0)
    key = lax.broadcasted_iota(jnp.int32, (96, 192), 1)
    same = window(40 * side + (query & 7)) == window((48 if side else -8) + (key & 7))
    value = jnp.zeros((96, 192), F32)
    for group in range(4):
        rows = (query >= 24 * group) & (query < 24 * group + 24)
        keys = (key >= 48 * group) & (key < 48 * group + 48)
        other = present if group % 2 == 0 else 1.0
        value = jnp.where(rows & keys & same, jnp.where(key < 48 * group + 24, 1.0, other), value)
    return jnp.concatenate([value] * 4, 0).astype(BF)


def head_blocks():
    row = lax.broadcasted_iota(jnp.int32, (256, 256), 0)
    lane = lax.broadcasted_iota(jnp.int32, (256, 256), 1)
    same = lax.shift_right_logical(row, 6) == lax.shift_right_logical(lane, 6)
    return jnp.where(same, 1.0, 0.0).astype(BF)


def attend_half(q, kown, vown, kpart, vpart, present, osum, wsum):
    ones = jnp.ones((192, 128), BF)
    heads = head_rows()
    for ch in range(2):
        mask = main_mask(ch, present)
        for lv in range(2):
            qs = jnp.concatenate([q[lv, r, 24 * ch : 24 * ch + 24] for r in range(3)], 0)
            cells = slice(16 * ch, 16 * ch + 32)
            for hg in range(2):
                feats = slice(256 * hg, 256 * hg + 256)
                k = jnp.concatenate([x[lv, r, cells, feats] for x in (kown, kpart) for r in range(3)], 0)
                v = jnp.concatenate([x[lv, r, cells, feats] for x in (vown, vpart) for r in range(3)], 0)
                o, w = scores_to_sums(qs[:, feats], k, v, mask, ones, heads)
                for r in range(3):
                    osum[lv, r, 24 * ch : 24 * ch + 24, feats] = o[24 * r : 24 * r + 24]
                    wsum[lv, r, 24 * ch : 24 * ch + 24, feats] = w[24 * r : 24 * r + 24]


def project(x_ref, lv, gain, weight, columns):
    normed = layer_norm(x_ref[lv].reshape(144, D).astype(F32), gain).astype(BF)
    return dot(normed, weight[:, columns])


def rows_kernel(tokens, near, far):
    start = 3 * lax.rem(lax.axis_index("lat"), 2)
    near[...] = tokens[:, pl.ds(3 - start, 3)]
    far[...] = tokens[:, pl.ds(start, 3)]


def own_kernel(
    xj, xi, ri, weight, gain, scales, qj, qi, kj, vj, osum, wsum, ki, vi, kr, vr
):
    block = head_blocks()
    lane = lax.broadcasted_iota(jnp.int32, (1, D), 1)
    scale = jnp.zeros((1, D), F32)
    for h in range(8):
        scale = jnp.where(lax.shift_right_logical(lane, 6) == h, scales[:, h : h + 1], scale)
    scale = scale * LOG2E
    for lv in range(2):
        for x, q, k, v in ((xi, qi, ki, vi), (xj, qj, kj, vj)):
            all3 = project(x, lv, gain[...], weight, slice(0, 1536))
            q[lv] = head_scaled(all3[:, :D], block, scale).reshape(3, 48, D)
            k[lv] = all3[:, D : 2 * D].astype(BF).reshape(3, 48, D)
            v[lv] = all3[:, 2 * D :].astype(BF).reshape(3, 48, D)
        both = project(ri, lv, gain[...], weight, slice(512, 1536))
        kr[lv] = both[:, :D].astype(BF).reshape(3, 48, D)
        vr[lv] = both[:, D:].astype(BF).reshape(3, 48, D)
    attend_half(qi, ki, vi, kr, vr, 1.0, osum, wsum)


def far_kernel(rj, weight, gain, qj, kj, vj, osum, wsum, kr, vr):
    for lv in range(2):
        both = project(rj, lv, gain[...], weight, slice(512, 1536))
        kr[lv] = both[:, :D].astype(BF).reshape(3, 48, D)
        vr[lv] = both[:, D:].astype(BF).reshape(3, 48, D)
    attend_half(qj, kj, vj, kr, vr, present_rows(), osum, wsum)


def last_kernel(
    left, right, xj, xi, qj, qi, oj, wj, oi, wi, qkv, gain,
    out_weight, merge_weight, merge_gain, split_weight, split_gain, out,
    attended, skip, fine,
):
    ones128 = jnp.ones((192, 128), BF)
    heads = head_rows()
    tops = (qj, qi)
    sums = ((oj, wj), (oi, wi))
    for half, (o, w) in enumerate(sums):
        attended[half, :, :, 8:40] = o[:, :, 8:40] * pl.reciprocal(w[:, :, 8:40], approx=True)
    for side, x in enumerate((left, right)):
        normed = layer_norm(x[...].astype(F32), gain[...]).astype(BF)
        both = dot(normed, qkv[:, D:])
        k = both[:, :D].astype(BF)
        v = both[:, D:].astype(BF)
        near = slice(40 * side, 40 * side + 8)
        q = jnp.concatenate(
            [tops[half][lv, r, near] for lv in range(2) for half in range(2) for r in range(3)], 0
        )
        sel = edge_mask(side, present_rows())
        for hg in range(2):
            feats = slice(256 * hg, 256 * hg + 256)
            oe, we = scores_to_sums(q[:, feats], k[:, feats], v[:, feats], sel, ones128, heads)
            at = 0
            for lv in range(2):
                for half, (o, w) in enumerate(sums):
                    for r in range(3):
                        whole = w[lv, r, near, feats] + we[at : at + 8]
                        part = o[lv, r, near, feats] + oe[at : at + 8]
                        attended[half, lv, r, near, feats] = part * pl.reciprocal(whole, approx=True)
                        at += 8
    for half, x in enumerate((xj, xi)):
        value = dot(attended[half].reshape(288, D).astype(BF), out_weight[...])
        value = x[...].reshape(288, D).astype(F32) + value
        value = value.astype(BF).astype(F32).reshape(2, 3, 48, D)
        for f in range(4):
            skip[half, :, :, f] = value[..., 128 * f : 128 * f + 128]
    parity = lax.rem(lax.axis_index("lat"), 2)
    groups = []
    for c in range(2):
        for r in range(2):
            pieces = []
            for lv in range(2):
                for a in range(3):
                    row = 2 * a + r
                    half = parity if row < 3 else 1 - parity
                    chunks = [skip[half, lv, row % 3, f, pl.ds(c, 24, stride=2), :] for f in range(4)]
                    pieces.append(jnp.concatenate(chunks, 1))
            groups.append(jnp.concatenate(pieces, 0))
    mean = sum(jnp.sum(g, -1, keepdims=True) for g in groups) * (1.0 / 2048)
    centered = [g - mean for g in groups]
    variance = sum(jnp.sum(g * g, -1, keepdims=True) for g in centered) * (1.0 / 2048)
    inverse = lax.rsqrt(variance + 1e-05)
    merged = jnp.concatenate(
        [
            (g * inverse * merge_gain[:, D * i : D * i + D]).astype(BF)
            for i, g in enumerate(centered)
        ],
        1,
    )
    coarse = dot(merged, merge_weight[...]).astype(BF)
    for c in range(2):
        for r in range(2):
            i = 2 * c + r
            expanded = dot(coarse, split_weight[:, D * i : D * i + D])
            done = groups[i] + layer_norm(expanded, split_gain[...])
            for lv in range(2):
                for a in range(3):
                    at = (lv * 3 + a) * 24
                    for f in range(4):
                        fine[lv, 2 * a + r, f, pl.ds(c, 24, stride=2), :] = done[
                            at : at + 24, 128 * f : 128 * f + 128
                        ]
    for f in range(4):
        out[:, :, :, 128 * f : 128 * f + 128] = fine[:, :, f].astype(BF)


def body(
    tokens,
    qkv_weight,
    out_weight,
    attn_gain,
    logit_scale,
    merge_weight,
    merge_gain,
    split_weight,
    split_gain,
):
    lats = lax.axis_size("lat")
    pair = [(i, i ^ 1) for i in range(lats)]
    cross = [(i, ((i + 1) ^ 1) - 1) for i in range(1, lats - 1)]

    def along(value, steps):
        count = lax.axis_size("lon")
        return lax.ppermute(value, "lon", [(i, (i + steps) % count) for i in range(count)])

    def cells(dtype):
        return jax.ShapeDtypeStruct((2, 3, 48, D), dtype)

    xi, xj = pl.pallas_call(
        rows_kernel,
        name="rows",
        out_shape=[cells(BF), cells(BF)],
        in_specs=[VMEM],
        out_specs=[VMEM] * 2,
        compiler_params=PARAMS,
        cost_estimate=pl.CostEstimate(flops=5 * 10**9, bytes_accessed=10**6, transcendentals=0),
    )(tokens)
    ri = lax.ppermute(xi, "lat", pair)
    rj_edge = lax.ppermute(jnp.concatenate([xj[:, :, :8], xj[:, :, 40:]], 2), "lat", cross)
    rj_mid = lax.ppermute(xj[:, :, 8:40], "lat", cross)

    def edge_cells(own, far):
        parts = [xj[:, :, own], rj_edge[:, :, far], xi[:, :, own], ri[:, :, own]]
        return jnp.concatenate(parts, 1).reshape(192, D)

    to_left = edge_cells(slice(0, 8), slice(0, 8))
    to_right = edge_cells(slice(40, 48), slice(8, 16))
    to_left, to_right, ri = lax.optimization_barrier((to_left, to_right, ri))
    left = along(to_right, 1)
    right = along(to_left, -1)

    gain = attn_gain.reshape(1, D)

    scratch = [pltpu.VMEM((2, 3, 48, D), BF)]
    qj, qi, kj, vj, oi, wi = pl.pallas_call(
        own_kernel,
        name="own_cells",
        out_shape=[cells(F32), cells(F32), cells(BF), cells(BF), cells(F32), cells(F32)],
        in_specs=[VMEM] * 6,
        out_specs=[VMEM] * 6,
        scratch_shapes=scratch * 4,
        compiler_params=PARAMS,
        cost_estimate=pl.CostEstimate(flops=3 * 10**9, bytes_accessed=4 * 10**6, transcendentals=10**6),
    )(xj, xi, ri, qkv_weight, gain, logit_scale.reshape(1, 8))
    rj_mid, qj = lax.optimization_barrier((rj_mid, qj))
    rj = jnp.concatenate([rj_edge[:, :, :8], rj_mid, rj_edge[:, :, 8:]], 2)
    oj, wj = pl.pallas_call(
        far_kernel,
        name="far_rows",
        out_shape=[cells(F32), cells(F32)],
        in_specs=[VMEM] * 6,
        out_specs=[VMEM] * 2,
        scratch_shapes=scratch * 2,
        compiler_params=PARAMS,
        cost_estimate=pl.CostEstimate(flops=2 * 10**9, bytes_accessed=4 * 10**6, transcendentals=10**6),
    )(rj, qkv_weight, gain, qj, kj, vj)
    return pl.pallas_call(
        last_kernel,
        name="edges_merge_split",
        out_shape=jax.ShapeDtypeStruct((2, 6, 48, D), BF),
        in_specs=[VMEM] * 17,
        out_specs=VMEM,
        scratch_shapes=[
            pltpu.VMEM((2, 2, 3, 48, D), F32),
            pltpu.VMEM((2, 2, 3, 4, 48, 128), F32),
            pltpu.VMEM((2, 6, 4, 48, 128), F32),
        ],
        compiler_params=PARAMS,
        cost_estimate=pl.CostEstimate(flops=3 * 10**9, bytes_accessed=12 * 10**6, transcendentals=10**6),
    )(
        left, right, xj, xi, qj, qi, oj, wj, oi, wi, qkv_weight, gain,
        out_weight, merge_weight, merge_gain.reshape(1, 4 * D), split_weight, split_gain.reshape(1, D),
    )


def solution(mesh):
    placed = (P(None, "lat", "lon", None), P(), P(), P(), P(), P(), P(), P(), P())
    return jax.shard_map(
        body, mesh=mesh, in_specs=placed, out_specs=P(None, "lat", "lon", None), check_vma=False
    )
```

```python
import jax
import jax.numpy as jnp
from jax import lax
from jax.experimental import pallas as pl
from jax.experimental.pallas import tpu as pltpu
from jax.sharding import PartitionSpec as P

BF = jnp.bfloat16
F32 = jnp.float32
D = 512
LOG2E = 1.4426950408889634
VMEM = pl.BlockSpec(memory_space=pltpu.VMEM)
PARAMS = pltpu.CompilerParams(vmem_limit_bytes=24 * 2**20)


def dot(a, b):
    return jnp.dot(a, b, preferred_element_type=F32)


def dot_t(a, b):
    return lax.dot_general(a, b, (((1,), (1,)), ((), ())), preferred_element_type=F32)


def layer_norm(value, gain):
    centered = value - jnp.mean(value, -1, keepdims=True)
    variance = jnp.mean(centered * centered, -1, keepdims=True)
    return centered * lax.rsqrt(variance + 1e-05) * gain


def head_scaled(value, block, extra=None):
    rounded = value.astype(BF)
    squares = rounded * rounded
    sums = jnp.concatenate([dot(squares[:, :256], block), dot(squares[:, 256:], block)], 1)
    inverse = lax.rsqrt(sums + 1e-06)
    return value * (inverse if extra is None else inverse * extra)


def stack_heads(q):
    lane = lax.broadcasted_iota(jnp.int32, q.shape, 1)
    return jnp.concatenate(
        [jnp.where((lane >= 64 * h) & (lane < 64 * h + 64), q, 0.0) for h in range(4)], 0
    ).astype(BF)


def unstack_heads(value, m):
    lane = lax.broadcasted_iota(jnp.int32, (m, 128), 1)
    halves = []
    for g in range(2):
        col = slice(128 * g, 128 * g + 128) if value.shape[1] > 1 else slice(None)
        first = value[2 * g * m : (2 * g + 1) * m, col]
        second = value[(2 * g + 1) * m : (2 * g + 2) * m, col]
        halves.append(jnp.where(lane < 64, first, second))
    return jnp.concatenate(halves, 1)


def scores_to_sums(q, k, v, mask):
    m = q.shape[0]
    weight = jnp.exp2(dot_t(stack_heads(q), k)) * mask
    total = jnp.sum(weight, 1, keepdims=True)
    return unstack_heads(dot(weight.astype(BF), v), m), unstack_heads(total, m)


def window(col):
    return lax.shift_right_logical((col + 18) * 5462, 16)


def present_rows():
    lat = lax.axis_index("lat")
    return jnp.where((lat > 0) & (lat < lax.axis_size("lat") - 1), 1.0, 0.0)


def main_mask(ch, present):
    query = lax.broadcasted_iota(jnp.int32, (72, 192), 0)
    key = lax.broadcasted_iota(jnp.int32, (72, 192), 1)
    row = (query >= 24).astype(jnp.int32) + (query >= 48).astype(jnp.int32)
    same = window(24 * ch + query - 24 * row) == window(16 * ch + (key & 31))
    value = jnp.where(same, jnp.where(key < 96, 1.0, present), 0.0)
    return jnp.concatenate([value] * 4, 0)


def edge_mask(side):
    query = lax.broadcasted_iota(jnp.int32, (96, 144), 0)
    key = lax.broadcasted_iota(jnp.int32, (96, 144), 1)
    same = window(40 * side + (query & 7)) == window((48 if side else -8) + (key & 7))
    keep = query < 0
    for group, (low, high) in enumerate(((0, 24), (72, 96), (24, 72), (96, 144))):
        rows = (query >= 24 * group) & (query < 24 * group + 24)
        keep = keep | (rows & (key >= low) & (key < high))
    return jnp.concatenate([jnp.where(same & keep, 1.0, 0.0)] * 4, 0)


def corner_mask(present):
    query = lax.broadcasted_iota(jnp.int32, (96, 96), 0)
    key = lax.broadcasted_iota(jnp.int32, (96, 96), 1)
    keep = query < 0
    for group in range(4):
        side = group // 2
        rows = (query >= 24 * group) & (query < 24 * group + 24)
        keys = (key >= 24 * group) & (key < 24 * group + 24)
        same = window(40 * side + (query & 7)) == window((48 if side else -8) + (key & 7))
        keep = keep | (rows & keys & same)
    return jnp.concatenate([jnp.where(keep, present, 0.0)] * 4, 0)


def head_blocks():
    row = lax.broadcasted_iota(jnp.int32, (256, 256), 0)
    lane = lax.broadcasted_iota(jnp.int32, (256, 256), 1)
    same = lax.shift_right_logical(row, 6) == lax.shift_right_logical(lane, 6)
    return jnp.where(same, 1.0, 0.0).astype(BF)


def attend_half(q, kown, vown, kpart, vpart, present, osum, wsum):
    for ch in range(2):
        mask = main_mask(ch, present)
        for lv in range(2):
            qs = jnp.concatenate([q[lv, r, 24 * ch : 24 * ch + 24] for r in range(3)], 0)
            cells = slice(16 * ch, 16 * ch + 32)
            for hg in range(2):
                feats = slice(256 * hg, 256 * hg + 256)
                k = jnp.concatenate([x[lv, r, cells, feats] for x in (kown, kpart) for r in range(3)], 0)
                v = jnp.concatenate([x[lv, r, cells, feats] for x in (vown, vpart) for r in range(3)], 0)
                o, w = scores_to_sums(qs[:, feats], k, v, mask)
                for r in range(3):
                    osum[lv, r, 24 * ch : 24 * ch + 24, feats] = o[24 * r : 24 * r + 24]
                    wsum[lv, r, 24 * ch : 24 * ch + 24, feats] = w[24 * r : 24 * r + 24]


def project(x_ref, lv, gain, weight, columns):
    normed = layer_norm(x_ref[lv].reshape(144, D).astype(F32), gain).astype(BF)
    return dot(normed, weight[:, columns])


def rows_kernel(tokens, near, far):
    start = 3 * lax.rem(lax.axis_index("lat"), 2)
    near[...] = tokens[:, pl.ds(3 - start, 3)]
    far[...] = tokens[:, pl.ds(start, 3)]


def own_kernel(
    xj, xi, ri, weight, gain, scales, qj, qi, kj, vj, osum, wsum, ki, vi, kr, vr
):
    block = head_blocks()
    lane = lax.broadcasted_iota(jnp.int32, (1, D), 1)
    scale = jnp.zeros((1, D), F32)
    for h in range(8):
        scale = jnp.where(lax.shift_right_logical(lane, 6) == h, scales[:, h : h + 1], scale)
    scale = scale * LOG2E
    for lv in range(2):
        for x, q, k, v in ((xi, qi, ki, vi), (xj, qj, kj, vj)):
            all3 = project(x, lv, gain[...], weight, slice(0, 1536))
            q[lv] = head_scaled(all3[:, :D], block, scale).reshape(3, 48, D)
            k[lv] = head_scaled(all3[:, D : 2 * D], block).astype(BF).reshape(3, 48, D)
            v[lv] = all3[:, 2 * D :].astype(BF).reshape(3, 48, D)
        both = project(ri, lv, gain[...], weight, slice(512, 1536))
        kr[lv] = head_scaled(both[:, :D], block).astype(BF).reshape(3, 48, D)
        vr[lv] = both[:, D:].astype(BF).reshape(3, 48, D)
    attend_half(qi, ki, vi, kr, vr, 1.0, osum, wsum)


def keys_values(tokens, qkv, gain, block):
    normed = layer_norm(tokens.astype(F32), gain).astype(BF)
    both = dot(normed, qkv[:, D:])
    return head_scaled(both[:, :D], block).astype(BF), both[:, D:].astype(BF)


def far_kernel(
    rj, left, right, xj, xi, qkv, gain, out_weight, qj, qi, kj, vj, oi, wi,
    skip, edge_sum, edge_weight, osum, wsum, kr, vr, attended,
):
    block = head_blocks()
    for lv in range(2):
        k, v = keys_values(rj[lv].reshape(144, D), qkv, gain[...], block)
        kr[lv] = k.reshape(3, 48, D)
        vr[lv] = v.reshape(3, 48, D)
    attend_half(qj, kj, vj, kr, vr, present_rows(), osum, wsum)
    mid = slice(8, 40)
    attended[:, :, mid] = oi[:, :, mid] * pl.reciprocal(wi[:, :, mid], approx=True)
    for side, x in enumerate((left, right)):
        k, v = keys_values(x[...], qkv, gain[...], block)
        near = slice(40 * side, 40 * side + 8)
        q = jnp.concatenate(
            [q[lv, r, near] for q in (qj, qi) for lv in range(2) for r in range(3)], 0
        )
        mask = edge_mask(side)
        for hg in range(2):
            feats = slice(256 * hg, 256 * hg + 256)
            oe, we = scores_to_sums(q[:, feats], k[:, feats], v[:, feats], mask)
            for lv in range(2):
                for r in range(3):
                    at = 24 * lv + 8 * r
                    to = slice(48 * side + at, 48 * side + at + 8)
                    edge_sum[to, feats] = osum[lv, r, near, feats] + oe[at : at + 8]
                    edge_weight[to, feats] = wsum[lv, r, near, feats] + we[at : at + 8]
                    total = oi[lv, r, near, feats] + oe[48 + at : 56 + at]
                    weight = wi[lv, r, near, feats] + we[48 + at : 56 + at]
                    attended[lv, r, near, feats] = total * pl.reciprocal(weight, approx=True)
    start = 3 * lax.rem(lax.axis_index("lat"), 2)
    whole = attended[...].reshape(288, D).astype(BF)
    value = xi[...].reshape(288, D).astype(F32) + dot(whole, out_weight[...])
    value = value.astype(BF).astype(F32).reshape(2, 3, 48, D)
    for f in range(4):
        skip[:, pl.ds(3 - start, 3), f] = value[..., 128 * f : 128 * f + 128]
    middle = osum[:, :, mid] * pl.reciprocal(wsum[:, :, mid], approx=True)
    value = dot(middle.reshape(192, D).astype(BF), out_weight[...]).reshape(2, 3, 32, D)
    value = (xj[...].astype(F32)[:, :, mid] + value).astype(BF).astype(F32)
    for f in range(4):
        skip[:, pl.ds(start, 3), f, mid] = value[..., 128 * f : 128 * f + 128]


def last_kernel(
    corners_left, corners_right, xj, qj, edge_sum, edge_weight, most, qkv, gain, out_weight,
    merge_weight, merge_gain, split_weight, split_gain, out, skip, fine, done_rows, sems,
):
    block = head_blocks()
    start = 3 * lax.rem(lax.axis_index("lat"), 2)
    corners = jnp.concatenate([corners_left[...], corners_right[...]], 0)
    k, v = keys_values(corners, qkv, gain[...], block)
    nears = [slice(40 * side, 40 * side + 8) for side in range(2)]
    spots = [(near, lv, r) for near in nears for lv in range(2) for r in range(3)]
    q = jnp.concatenate([qj[lv, r, near] for near, lv, r in spots], 0)
    mask = corner_mask(present_rows())
    attended = []
    for hg in range(2):
        feats = slice(256 * hg, 256 * hg + 256)
        oc, wc = scores_to_sums(q[:, feats], k[:, feats], v[:, feats], mask)
        weight = edge_weight[:, feats] + wc
        attended.append((edge_sum[:, feats] + oc) * pl.reciprocal(weight, approx=True))
    value = dot(jnp.concatenate(attended, 1).astype(BF), out_weight[...])
    own = xj[...].astype(F32)
    skip[...] = most[...]
    for i, (near, lv, r) in enumerate(spots):
        cell = (own[lv, r, near] + value[8 * i : 8 * i + 8]).astype(BF).astype(F32)
        for f in range(4):
            skip[lv, start + r, f, near] = cell[:, 128 * f : 128 * f + 128]
    groups = []
    for c in range(2):
        for r in range(2):
            pieces = []
            for lv in range(2):
                for a in range(3):
                    chunks = [skip[lv, 2 * a + r, f, pl.ds(c, 24, stride=2), :] for f in range(4)]
                    pieces.append(jnp.concatenate(chunks, 1))
            groups.append(jnp.concatenate(pieces, 0))
    mean = sum(jnp.sum(g, -1, keepdims=True) for g in groups) * (1.0 / 2048)
    centered = [g - mean for g in groups]
    variance = sum(jnp.sum(g * g, -1, keepdims=True) for g in centered) * (1.0 / 2048)
    inverse = lax.rsqrt(variance + 1e-05)
    merged = jnp.concatenate(
        [
            (g * inverse * merge_gain[:, D * i : D * i + D]).astype(BF)
            for i, g in enumerate(centered)
        ],
        1,
    )
    coarse = dot(merged, merge_weight[...]).astype(BF)
    copies = []
    for r in range(2):
        for c in range(2):
            i = 2 * c + r
            expanded = dot(coarse, split_weight[:, D * i : D * i + D])
            done = groups[i] + layer_norm(expanded, split_gain[...])
            for lv in range(2):
                for a in range(3):
                    at = (lv * 3 + a) * 24
                    for f in range(4):
                        fine[lv, 2 * a + r, f, pl.ds(c, 24, stride=2), :] = done[
                            at : at + 24, 128 * f : 128 * f + 128
                        ]
        for a in range(3):
            row = 2 * a + r
            for f in range(4):
                done_rows[:, row, :, 128 * f : 128 * f + 128] = fine[:, row, f].astype(BF)
            copies.append(pltpu.make_async_copy(done_rows.at[:, row], out.at[:, row], sems.at[row]))
            copies[-1].start()
    for copy in copies:
        copy.wait()


def body(
    tokens,
    qkv_weight,
    out_weight,
    attn_gain,
    logit_scale,
    merge_weight,
    merge_gain,
    split_weight,
    split_gain,
):
    lats = lax.axis_size("lat")
    pair = [(i, i ^ 1) for i in range(lats)]
    cross = [(i, ((i + 1) ^ 1) - 1) for i in range(1, lats - 1)]

    def along(value, steps):
        count = lax.axis_size("lon")
        return lax.ppermute(value, "lon", [(i, (i + steps) % count) for i in range(count)])

    def cells(dtype):
        return jax.ShapeDtypeStruct((2, 3, 48, D), dtype)

    xi, xj = pl.pallas_call(
        rows_kernel,
        name="rows",
        out_shape=[cells(BF), cells(BF)],
        in_specs=[VMEM],
        out_specs=[VMEM] * 2,
        compiler_params=PARAMS,
        cost_estimate=pl.CostEstimate(flops=5 * 10**9, bytes_accessed=10**6, transcendentals=0),
    )(tokens)
    ri = lax.ppermute(xi, "lat", pair)
    rj = lax.ppermute(xj, "lat", cross)

    def edge_cells(own):
        return jnp.concatenate([xj[:, :, own], xi[:, :, own], ri[:, :, own]], 1).reshape(144, D)

    first, final = slice(0, 8), slice(40, 48)
    to_left, to_right, ri = lax.optimization_barrier((edge_cells(first), edge_cells(final), ri))
    left = along(to_right, 1)
    right = along(to_left, -1)
    gain = attn_gain.reshape(1, D)

    scratch = [pltpu.VMEM((2, 3, 48, D), BF)]
    qj, qi, kj, vj, oi, wi = pl.pallas_call(
        own_kernel,
        name="own_cells",
        out_shape=[cells(F32), cells(F32), cells(BF), cells(BF), cells(F32), cells(F32)],
        in_specs=[VMEM] * 6,
        out_specs=[VMEM] * 6,
        scratch_shapes=scratch * 4,
        compiler_params=PARAMS,
        cost_estimate=pl.CostEstimate(flops=3 * 10**9, bytes_accessed=4 * 10**6, transcendentals=10**6),
    )(xj, xi, ri, qkv_weight, gain, logit_scale.reshape(1, 8))
    corner_left, corner_right, rj, qj = lax.optimization_barrier(
        (rj[:, :, first].reshape(48, D), rj[:, :, final].reshape(48, D), rj, qj)
    )
    corners_left = along(corner_right, 1)
    corners_right = along(corner_left, -1)
    flat = jax.ShapeDtypeStruct((96, D), F32)
    chunked = jax.ShapeDtypeStruct((2, 6, 4, 48, 128), F32)
    most, edge_sum, edge_weight = pl.pallas_call(
        far_kernel,
        name="far_rows_and_edges",
        out_shape=[chunked, flat, flat],
        in_specs=[VMEM] * 14,
        out_specs=[VMEM] * 3,
        scratch_shapes=[pltpu.VMEM((2, 3, 48, D), F32)] * 2
        + [pltpu.VMEM((2, 3, 48, D), BF)] * 2
        + [pltpu.VMEM((2, 3, 48, D), F32)],
        compiler_params=PARAMS,
        cost_estimate=pl.CostEstimate(flops=3 * 10**9, bytes_accessed=4 * 10**6, transcendentals=10**6),
    )(rj, left, right, xj, xi, qkv_weight, gain, out_weight, qj, qi, kj, vj, oi, wi)
    return pl.pallas_call(
        last_kernel,
        name="corners_merge_split",
        out_shape=jax.ShapeDtypeStruct((2, 6, 48, D), BF),
        in_specs=[VMEM] * 14,
        out_specs=pl.BlockSpec(memory_space=pl.ANY),
        scratch_shapes=[
            pltpu.VMEM((2, 6, 4, 48, 128), F32),
            pltpu.VMEM((2, 6, 4, 48, 128), F32),
            pltpu.VMEM((2, 6, 48, D), BF),
            pltpu.SemaphoreType.DMA((6,)),
        ],
        compiler_params=PARAMS,
        cost_estimate=pl.CostEstimate(flops=3 * 10**9, bytes_accessed=12 * 10**6, transcendentals=10**6),
    )(
        corners_left, corners_right, xj, qj, edge_sum, edge_weight, most, qkv_weight, gain, out_weight,
        merge_weight, merge_gain.reshape(1, 4 * D), split_weight, split_gain.reshape(1, D),
    )


def solution(mesh):
    placed = (P(None, "lat", "lon", None), P(), P(), P(), P(), P(), P(), P(), P())
    return jax.shard_map(
        body, mesh=mesh, in_specs=placed, out_specs=P(None, "lat", "lon", None), check_vma=False
    )
```

```python
import jax
import jax.numpy as jnp
from jax import lax
from jax.experimental import pallas as pl
from jax.experimental.pallas import tpu as pltpu
from jax.sharding import PartitionSpec as P

BF = jnp.bfloat16
F32 = jnp.float32
D = 512
LOG2E = 1.4426950408889634
VMEM = pl.BlockSpec(memory_space=pltpu.VMEM)
PARAMS = pltpu.CompilerParams(vmem_limit_bytes=24 * 2**20)


def dot(a, b):
    return jnp.dot(a, b, preferred_element_type=F32)


def dot_t(a, b):
    return lax.dot_general(a, b, (((1,), (1,)), ((), ())), preferred_element_type=F32)


def layer_norm(value, gain):
    centered = value - jnp.mean(value, -1, keepdims=True)
    variance = jnp.mean(centered * centered, -1, keepdims=True)
    return centered * lax.rsqrt(variance + 1e-05) * gain


def head_scaled(value, block, extra=None):
    rounded = value.astype(BF)
    squares = rounded * rounded
    sums = jnp.concatenate([dot(squares[:, :256], block), dot(squares[:, 256:], block)], 1)
    inverse = lax.rsqrt(sums + 1e-06)
    return value * (inverse if extra is None else inverse * extra)


def stack_heads(q):
    lane = lax.broadcasted_iota(jnp.int32, q.shape, 1)
    return jnp.concatenate(
        [jnp.where((lane >= 64 * h) & (lane < 64 * h + 64), q, 0.0) for h in range(4)], 0
    ).astype(BF)


def unstack_heads(value, m):
    lane = lax.broadcasted_iota(jnp.int32, (m, 128), 1)
    halves = []
    for g in range(2):
        col = slice(128 * g, 128 * g + 128) if value.shape[1] > 1 else slice(None)
        first = value[2 * g * m : (2 * g + 1) * m, col]
        second = value[(2 * g + 1) * m : (2 * g + 2) * m, col]
        halves.append(jnp.where(lane < 64, first, second))
    return jnp.concatenate(halves, 1)


def scores_to_sums(q, k, v, mask):
    m = q.shape[0]
    weight = jnp.exp2(dot_t(stack_heads(q), k)) * mask
    total = jnp.sum(weight, 1, keepdims=True)
    return unstack_heads(dot(weight.astype(BF), v), m), unstack_heads(total, m)


def window(col):
    return lax.shift_right_logical((col + 18) * 5462, 16)


def present_rows():
    lat = lax.axis_index("lat")
    return jnp.where((lat > 0) & (lat < lax.axis_size("lat") - 1), 1.0, 0.0)


def window_mask(ch, lv, near, present):
    query = lax.broadcasted_iota(jnp.int32, (72, 240), 0)
    key = lax.broadcasted_iota(jnp.int32, (72, 240), 1)
    row = (query >= 24).astype(jnp.int32) + (query >= 48).astype(jnp.int32)
    edge = key >= 192
    column = jnp.where(edge, (48 if ch else -8) + (key & 7), 16 * ch + (key & 31))
    same = window(24 * ch + query - 24 * row) == window(column)
    if near:
        value = jnp.where(same, 1.0, 0.0)
    else:
        other = (key >= 96) & (key < 192)
        level = (key < 216) if lv == 0 else (key < 192) | (key >= 216)
        value = jnp.where(same & level, jnp.where(other, present, 1.0), 0.0)
    return jnp.concatenate([value] * 4, 0)


def corner_mask(present):
    query = lax.broadcasted_iota(jnp.int32, (96, 96), 0)
    key = lax.broadcasted_iota(jnp.int32, (96, 96), 1)
    keep = query < 0
    for group in range(4):
        side = group // 2
        rows = (query >= 24 * group) & (query < 24 * group + 24)
        keys = (key >= 24 * group) & (key < 24 * group + 24)
        same = window(40 * side + (query & 7)) == window((48 if side else -8) + (key & 7))
        keep = keep | (rows & keys & same)
    return jnp.concatenate([jnp.where(keep, present, 0.0)] * 4, 0)


def head_blocks():
    row = lax.broadcasted_iota(jnp.int32, (256, 256), 0)
    lane = lax.broadcasted_iota(jnp.int32, (256, 256), 1)
    same = lax.shift_right_logical(row, 6) == lax.shift_right_logical(lane, 6)
    return jnp.where(same, 1.0, 0.0).astype(BF)


def attend_half(q, kown, vown, kpart, vpart, kedge, vedge, near, present, store):
    for ch in range(2):
        for lv in range(2):
            mask = window_mask(ch, lv, near, present)
            qs = jnp.concatenate([q[lv, r, 24 * ch : 24 * ch + 24] for r in range(3)], 0)
            cells = slice(16 * ch, 16 * ch + 32)
            edge = slice(48 * lv, 48 * lv + 48) if near else slice(96, 144)
            for hg in range(2):
                feats = slice(256 * hg, 256 * hg + 256)
                k = [x[lv, r, cells, feats] for x in (kown, kpart) for r in range(3)]
                v = [x[lv, r, cells, feats] for x in (vown, vpart) for r in range(3)]
                k = jnp.concatenate(k + [kedge[ch, edge, feats]], 0)
                v = jnp.concatenate(v + [vedge[ch, edge, feats]], 0)
                o, w = scores_to_sums(qs[:, feats], k, v, mask)
                for r in range(3):
                    rows = slice(24 * r, 24 * r + 24)
                    store(lv, r, slice(24 * ch, 24 * ch + 24), feats, o[rows], w[rows])


def project(x_ref, lv, gain, weight, columns):
    normed = layer_norm(x_ref[lv].reshape(144, D).astype(F32), gain).astype(BF)
    return dot(normed, weight[:, columns])


def rows_kernel(tokens, near, far):
    start = 3 * lax.rem(lax.axis_index("lat"), 2)
    near[...] = tokens[:, pl.ds(3 - start, 3)]
    far[...] = tokens[:, pl.ds(start, 3)]


def own_kernel(xj, xi, ri, weight, gain, scales, qj, qi, kj, vj, ki, vi, kr, vr):
    block = head_blocks()
    lane = lax.broadcasted_iota(jnp.int32, (1, D), 1)
    scale = jnp.zeros((1, D), F32)
    for h in range(8):
        scale = jnp.where(lax.shift_right_logical(lane, 6) == h, scales[:, h : h + 1], scale)
    scale = scale * LOG2E
    for lv in range(2):
        for x, q, k, v in ((xi, qi, ki, vi), (xj, qj, kj, vj)):
            all3 = project(x, lv, gain[...], weight, slice(0, 1536))
            q[lv] = head_scaled(all3[:, :D], block, scale).reshape(3, 48, D)
            k[lv] = head_scaled(all3[:, D : 2 * D], block).astype(BF).reshape(3, 48, D)
            v[lv] = all3[:, 2 * D :].astype(BF).reshape(3, 48, D)
        both = project(ri, lv, gain[...], weight, slice(512, 1536))
        kr[lv] = head_scaled(both[:, :D], block).astype(BF).reshape(3, 48, D)
        vr[lv] = both[:, D:].astype(BF).reshape(3, 48, D)


def keys_values(tokens, qkv, gain, block):
    normed = layer_norm(tokens.astype(F32), gain).astype(BF)
    both = dot(normed, qkv[:, D:])
    return head_scaled(both[:, :D], block).astype(BF), both[:, D:].astype(BF)


def far_kernel(
    rj, left, right, xj, xi, qkv, gain, out_weight, qj, qi, kj, vj, ki, vi, kn, vn,
    skip, edge_sum, edge_weight, osum, wsum, kr, vr, ke, ve, attended,
):
    block = head_blocks()
    mid = slice(8, 40)
    for side, x in enumerate((left, right)):
        ke[side], ve[side] = keys_values(x[...], qkv, gain[...], block)
    for lv in range(2):
        k, v = keys_values(rj[lv].reshape(144, D), qkv, gain[...], block)
        kr[lv] = k.reshape(3, 48, D)
        vr[lv] = v.reshape(3, 48, D)

    def finish(lv, r, columns, feats, o, w):
        attended[lv, r, columns, feats] = o * pl.reciprocal(w, approx=True)

    def keep(lv, r, columns, feats, o, w):
        osum[lv, r, columns, feats] = o
        wsum[lv, r, columns, feats] = w

    attend_half(qi, ki, vi, kn, vn, ke, ve, True, 1.0, finish)
    attend_half(qj, kj, vj, kr, vr, ke, ve, False, present_rows(), keep)
    for side in range(2):
        near = slice(40 * side, 40 * side + 8)
        for lv in range(2):
            for r in range(3):
                to = slice(48 * side + 24 * lv + 8 * r, 48 * side + 24 * lv + 8 * r + 8)
                edge_sum[to] = osum[lv, r, near]
                edge_weight[to] = wsum[lv, r, near]
    start = 3 * lax.rem(lax.axis_index("lat"), 2)
    whole = attended[...].reshape(288, D).astype(BF)
    value = xi[...].reshape(288, D).astype(F32) + dot(whole, out_weight[...])
    value = value.astype(BF).astype(F32).reshape(2, 3, 48, D)
    for f in range(4):
        skip[:, pl.ds(3 - start, 3), f] = value[..., 128 * f : 128 * f + 128]
    middle = osum[:, :, mid] * pl.reciprocal(wsum[:, :, mid], approx=True)
    value = dot(middle.reshape(192, D).astype(BF), out_weight[...]).reshape(2, 3, 32, D)
    value = (xj[...].astype(F32)[:, :, mid] + value).astype(BF).astype(F32)
    for f in range(4):
        skip[:, pl.ds(start, 3), f, mid] = value[..., 128 * f : 128 * f + 128]


def last_kernel(
    corners_left, corners_right, xj, qj, edge_sum, edge_weight, most, qkv, gain, out_weight,
    merge_weight, merge_gain, split_weight, split_gain, out, skip, fine, done_rows, sems,
):
    block = head_blocks()
    start = 3 * lax.rem(lax.axis_index("lat"), 2)
    corners = jnp.concatenate([corners_left[...], corners_right[...]], 0)
    k, v = keys_values(corners, qkv, gain[...], block)
    nears = [slice(40 * side, 40 * side + 8) for side in range(2)]
    spots = [(near, lv, r) for near in nears for lv in range(2) for r in range(3)]
    q = jnp.concatenate([qj[lv, r, near] for near, lv, r in spots], 0)
    mask = corner_mask(present_rows())
    attended = []
    for hg in range(2):
        feats = slice(256 * hg, 256 * hg + 256)
        oc, wc = scores_to_sums(q[:, feats], k[:, feats], v[:, feats], mask)
        weight = edge_weight[:, feats] + wc
        attended.append((edge_sum[:, feats] + oc) * pl.reciprocal(weight, approx=True))
    value = dot(jnp.concatenate(attended, 1).astype(BF), out_weight[...])
    own = xj[...].astype(F32)
    skip[...] = most[...]
    for i, (near, lv, r) in enumerate(spots):
        cell = (own[lv, r, near] + value[8 * i : 8 * i + 8]).astype(BF).astype(F32)
        for f in range(4):
            skip[lv, start + r, f, near] = cell[:, 128 * f : 128 * f + 128]
    groups = []
    for c in range(2):
        for r in range(2):
            pieces = []
            for lv in range(2):
                for a in range(3):
                    chunks = [skip[lv, 2 * a + r, f, pl.ds(c, 24, stride=2), :] for f in range(4)]
                    pieces.append(jnp.concatenate(chunks, 1))
            groups.append(jnp.concatenate(pieces, 0))
    mean = sum(jnp.sum(g, -1, keepdims=True) for g in groups) * (1.0 / 2048)
    centered = [g - mean for g in groups]
    variance = sum(jnp.sum(g * g, -1, keepdims=True) for g in centered) * (1.0 / 2048)
    inverse = lax.rsqrt(variance + 1e-05)
    coarse = 0.0
    for i, g in enumerate(centered):
        part = slice(D * i, D * i + D)
        normed = (g * inverse * merge_gain[:, part]).astype(BF)
        coarse = coarse + dot(normed, merge_weight[part])
    coarse = coarse.astype(BF)
    copies = []
    for r in range(2):
        for c in range(2):
            i = 2 * c + r
            expanded = dot(coarse, split_weight[:, D * i : D * i + D])
            done = groups[i] + layer_norm(expanded, split_gain[...])
            for lv in range(2):
                for a in range(3):
                    at = (lv * 3 + a) * 24
                    for f in range(4):
                        fine[lv, 2 * a + r, f, pl.ds(c, 24, stride=2), :] = done[
                            at : at + 24, 128 * f : 128 * f + 128
                        ]
        for lv in range(2):
            for a in range(3):
                row = 2 * a + r
                for f in range(4):
                    done_rows[lv, row, :, 128 * f : 128 * f + 128] = fine[lv, row, f].astype(BF)
                at = (lv, row)
                copies.append(
                    pltpu.make_async_copy(done_rows.at[at], out.at[at], sems.at[lv, row])
                )
                copies[-1].start()
    for copy in copies:
        copy.wait()


def body(
    tokens,
    qkv_weight,
    out_weight,
    attn_gain,
    logit_scale,
    merge_weight,
    merge_gain,
    split_weight,
    split_gain,
):
    lats = lax.axis_size("lat")
    pair = [(i, i ^ 1) for i in range(lats)]
    cross = [(i, ((i + 1) ^ 1) - 1) for i in range(1, lats - 1)]

    def along(value, steps):
        count = lax.axis_size("lon")
        return lax.ppermute(value, "lon", [(i, (i + steps) % count) for i in range(count)])

    def cells(dtype):
        return jax.ShapeDtypeStruct((2, 3, 48, D), dtype)

    xi, xj = pl.pallas_call(
        rows_kernel,
        name="rows",
        out_shape=[cells(BF), cells(BF)],
        in_specs=[VMEM],
        out_specs=[VMEM] * 2,
        compiler_params=PARAMS,
        cost_estimate=pl.CostEstimate(flops=5 * 10**9, bytes_accessed=10**6, transcendentals=0),
    )(tokens)
    ri = lax.ppermute(xi, "lat", pair)
    rj = lax.ppermute(xj, "lat", cross)

    def edge_cells(own):
        near = jnp.concatenate([xi[:, :, own], ri[:, :, own]], 1).reshape(96, D)
        return jnp.concatenate([near, xj[:, :, own].reshape(48, D)], 0)

    first, final = slice(0, 8), slice(40, 48)
    to_left, to_right, ri = lax.optimization_barrier((edge_cells(first), edge_cells(final), ri))
    left = along(to_right, 1)
    right = along(to_left, -1)
    gain = attn_gain.reshape(1, D)

    qj, qi, kj, vj, ki, vi, kn, vn = pl.pallas_call(
        own_kernel,
        name="own_cells",
        out_shape=[cells(F32)] * 2 + [cells(BF)] * 6,
        in_specs=[VMEM] * 6,
        out_specs=[VMEM] * 8,
        compiler_params=PARAMS,
        cost_estimate=pl.CostEstimate(flops=3 * 10**9, bytes_accessed=4 * 10**6, transcendentals=10**6),
    )(xj, xi, ri, qkv_weight, gain, logit_scale.reshape(1, 8))
    corner_left, corner_right, rj, qj = lax.optimization_barrier(
        (rj[:, :, first].reshape(48, D), rj[:, :, final].reshape(48, D), rj, qj)
    )
    corners_left = along(corner_right, 1)
    corners_right = along(corner_left, -1)
    flat = jax.ShapeDtypeStruct((96, D), F32)
    chunked = jax.ShapeDtypeStruct((2, 6, 4, 48, 128), F32)
    most, edge_sum, edge_weight = pl.pallas_call(
        far_kernel,
        name="far_rows_and_edges",
        out_shape=[chunked, flat, flat],
        in_specs=[VMEM] * 16,
        out_specs=[VMEM] * 3,
        scratch_shapes=[pltpu.VMEM((2, 3, 48, D), F32)] * 2
        + [pltpu.VMEM((2, 3, 48, D), BF)] * 2
        + [pltpu.VMEM((2, 144, D), BF)] * 2
        + [pltpu.VMEM((2, 3, 48, D), F32)],
        compiler_params=PARAMS,
        cost_estimate=pl.CostEstimate(flops=5 * 10**8, bytes_accessed=4 * 10**6, transcendentals=10**6),
    )(rj, left, right, xj, xi, qkv_weight, gain, out_weight, qj, qi, kj, vj, ki, vi, kn, vn)
    return pl.pallas_call(
        last_kernel,
        name="corners_merge_split",
        out_shape=jax.ShapeDtypeStruct((2, 6, 48, D), BF),
        in_specs=[VMEM] * 14,
        out_specs=pl.BlockSpec(memory_space=pl.ANY),
        scratch_shapes=[
            pltpu.VMEM((2, 6, 4, 48, 128), F32),
            pltpu.VMEM((2, 6, 4, 48, 128), F32),
            pltpu.VMEM((2, 6, 48, D), BF),
            pltpu.SemaphoreType.DMA((2, 6)),
        ],
        compiler_params=PARAMS,
        cost_estimate=pl.CostEstimate(flops=3 * 10**9, bytes_accessed=12 * 10**6, transcendentals=10**6),
    )(
        corners_left, corners_right, xj, qj, edge_sum, edge_weight, most, qkv_weight, gain, out_weight,
        merge_weight, merge_gain.reshape(1, 4 * D), split_weight, split_gain.reshape(1, D),
    )


def solution(mesh):
    placed = (P(None, "lat", "lon", None), P(), P(), P(), P(), P(), P(), P(), P())
    return jax.shard_map(
        body, mesh=mesh, in_specs=placed, out_specs=P(None, "lat", "lon", None), check_vma=False
    )
```

```python
import jax
import jax.numpy as jnp
from jax import lax
from jax.experimental import pallas as pl
from jax.experimental.pallas import tpu as pltpu
from jax.sharding import PartitionSpec as P

BF = jnp.bfloat16
F32 = jnp.float32
D = 512
LOG2E = 1.4426950408889634
VMEM = pl.BlockSpec(memory_space=pltpu.VMEM)
PARAMS = pltpu.CompilerParams(vmem_limit_bytes=24 * 2**20)


def dot(a, b):
    return jnp.dot(a, b, preferred_element_type=F32)


def dot_t(a, b):
    return lax.dot_general(a, b, (((1,), (1,)), ((), ())), preferred_element_type=F32)


def layer_norm(value, gain):
    centered = value - jnp.mean(value, -1, keepdims=True)
    variance = jnp.mean(centered * centered, -1, keepdims=True)
    return centered * lax.rsqrt(variance + 1e-05) * gain


def head_scaled(value, block, extra=None):
    rounded = value.astype(BF)
    squares = rounded * rounded
    sums = jnp.concatenate([dot(squares[:, :256], block), dot(squares[:, 256:], block)], 1)
    inverse = lax.rsqrt(sums + 1e-06)
    return value * (inverse if extra is None else inverse * extra)


def stack_heads(q):
    lane = lax.broadcasted_iota(jnp.int32, q.shape, 1)
    return jnp.concatenate(
        [jnp.where((lane >= 64 * h) & (lane < 64 * h + 64), q, 0.0) for h in range(4)], 0
    ).astype(BF)


def unstack_heads(value, m):
    lane = lax.broadcasted_iota(jnp.int32, (m, 128), 1)
    halves = []
    for g in range(2):
        col = slice(128 * g, 128 * g + 128) if value.shape[1] > 1 else slice(None)
        first = value[2 * g * m : (2 * g + 1) * m, col]
        second = value[(2 * g + 1) * m : (2 * g + 2) * m, col]
        halves.append(jnp.where(lane < 64, first, second))
    return jnp.concatenate(halves, 1)


def scores_to_sums(q, k, v, mask):
    m = q.shape[0]
    weight = jnp.exp2(dot_t(stack_heads(q), k)) * mask
    total = jnp.sum(weight, 1, keepdims=True)
    return unstack_heads(dot(weight.astype(BF), v), m), unstack_heads(total, m)


def window(col):
    return lax.shift_right_logical((col + 18) * 5462, 16)


def present_rows():
    lat = lax.axis_index("lat")
    return jnp.where((lat > 0) & (lat < lax.axis_size("lat") - 1), 1.0, 0.0)


def window_mask(ch):
    query = lax.broadcasted_iota(jnp.int32, (72, 240), 0)
    key = lax.broadcasted_iota(jnp.int32, (72, 240), 1)
    row = (query >= 24).astype(jnp.int32) + (query >= 48).astype(jnp.int32)
    column = jnp.where(key >= 192, (48 if ch else -8) + (key & 7), 16 * ch + (key & 31))
    same = window(24 * ch + query - 24 * row) == window(column)
    return jnp.where(same, 1.0, 0.0)


def far_keys(lv, present):
    key = lax.broadcasted_iota(jnp.int32, (1, 240), 1)
    level = (key < 216) if lv == 0 else (key < 192) | (key >= 216)
    other = (key >= 96) & (key < 192)
    return jnp.where(level, jnp.where(other, present, 1.0), 0.0)


def corner_mask(present):
    query = lax.broadcasted_iota(jnp.int32, (96, 96), 0)
    key = lax.broadcasted_iota(jnp.int32, (96, 96), 1)
    group = lax.shift_right_logical(query * 2731, 16) == lax.shift_right_logical(key * 2731, 16)
    query = jnp.where(query >= 48, 40, 0) + (query & 7)
    key = jnp.where(key >= 48, 48, -8) + (key & 7)
    same = window(query) == window(key)
    return jnp.concatenate([jnp.where(same & group, present, 0.0)] * 4, 0)


def head_blocks():
    row = lax.broadcasted_iota(jnp.int32, (256, 256), 0)
    lane = lax.broadcasted_iota(jnp.int32, (256, 256), 1)
    same = lax.shift_right_logical(row, 6) == lax.shift_right_logical(lane, 6)
    return jnp.where(same, 1.0, 0.0).astype(BF)


def attend_half(q, kown, vown, kpart, vpart, kedge, vedge, near, present, store):
    for ch in range(2):
        base = window_mask(ch)
        for lv in range(2):
            mask = base if near else base * far_keys(lv, present)
            mask = jnp.concatenate([mask] * 4, 0)
            qs = jnp.concatenate([q[lv, r, 24 * ch : 24 * ch + 24] for r in range(3)], 0)
            cells = slice(16 * ch, 16 * ch + 32)
            edge = slice(48 * lv, 48 * lv + 48) if near else slice(96, 144)
            for hg in range(2):
                feats = slice(256 * hg, 256 * hg + 256)
                k = [x[lv, r, cells, feats] for x in (kown, kpart) for r in range(3)]
                v = [x[lv, r, cells, feats] for x in (vown, vpart) for r in range(3)]
                k = jnp.concatenate(k + [kedge[ch, edge, feats]], 0)
                v = jnp.concatenate(v + [vedge[ch, edge, feats]], 0)
                o, w = scores_to_sums(qs[:, feats], k, v, mask)
                for r in range(3):
                    rows = slice(24 * r, 24 * r + 24)
                    store(lv, r, slice(24 * ch, 24 * ch + 24), feats, o[rows], w[rows])


def project(x_ref, lv, gain, weight, columns):
    normed = layer_norm(x_ref[lv].reshape(144, D).astype(F32), gain).astype(BF)
    return dot(normed, weight[:, columns])


def rows_kernel(tokens, far, near):
    start = 3 * lax.rem(lax.axis_index("lat"), 2)
    near[...] = tokens[:, pl.ds(3 - start, 3)]
    far[...] = tokens[:, pl.ds(start, 3)]


def head_scale(scales):
    lane = lax.broadcasted_iota(jnp.int32, (1, D), 1)
    scale = jnp.zeros((1, D), F32)
    for h in range(8):
        scale = jnp.where(lax.shift_right_logical(lane, 6) == h, scales[:, h : h + 1], scale)
    return scale * LOG2E


def own_half(x, weight, gain, scale, block, q, k, v):
    for lv in range(2):
        all3 = project(x, lv, gain, weight, slice(0, 1536))
        q[lv] = head_scaled(all3[:, :D], block, scale).reshape(3, 48, D)
        k[lv] = head_scaled(all3[:, D : 2 * D], block).astype(BF).reshape(3, 48, D)
        v[lv] = all3[:, 2 * D :].astype(BF).reshape(3, 48, D)


def own_kernel(xj, weight, gain, scales, qj, kj, vj):
    own_half(xj, weight, gain[...], head_scale(scales), head_blocks(), qj, kj, vj)


def near_kernel(xi, ri, weight, gain, scales, qi, ki, vi, kr, vr):
    block = head_blocks()
    own_half(xi, weight, gain[...], head_scale(scales), block, qi, ki, vi)
    for lv in range(2):
        k, v = keys_values(ri[lv].reshape(144, D), weight, gain[...], block)
        kr[lv] = k.reshape(3, 48, D)
        vr[lv] = v.reshape(3, 48, D)


def keys_values(tokens, qkv, gain, block):
    normed = layer_norm(tokens.astype(F32), gain).astype(BF)
    both = dot(normed, qkv[:, D:])
    return head_scaled(both[:, :D], block).astype(BF), both[:, D:].astype(BF)


def far_kernel(
    rj, left, right, xj, xi, qkv, gain, out_weight, qj, qi, kj, vj, ki, vi, kn, vn,
    skip, edge_sum, edge_weight, osum, wsum, kr, vr, ke, ve, attended,
):
    block = head_blocks()
    mid = slice(8, 40)
    for side, x in enumerate((left, right)):
        ke[side], ve[side] = keys_values(x[...], qkv, gain[...], block)
    for lv in range(2):
        k, v = keys_values(rj[lv].reshape(144, D), qkv, gain[...], block)
        kr[lv] = k.reshape(3, 48, D)
        vr[lv] = v.reshape(3, 48, D)

    def finish(lv, r, columns, feats, o, w):
        attended[lv, r, columns, feats] = o * pl.reciprocal(w, approx=True)

    def keep(lv, r, columns, feats, o, w):
        osum[lv, r, columns, feats] = o
        wsum[lv, r, columns, feats] = w

    attend_half(qi, ki, vi, kn, vn, ke, ve, True, 1.0, finish)
    attend_half(qj, kj, vj, kr, vr, ke, ve, False, present_rows(), keep)
    for side in range(2):
        near = slice(40 * side, 40 * side + 8)
        for lv in range(2):
            for r in range(3):
                to = slice(48 * side + 24 * lv + 8 * r, 48 * side + 24 * lv + 8 * r + 8)
                edge_sum[to] = osum[lv, r, near]
                edge_weight[to] = wsum[lv, r, near]
    start = 3 * lax.rem(lax.axis_index("lat"), 2)
    whole = attended[...].reshape(288, D).astype(BF)
    value = xi[...].reshape(288, D).astype(F32) + dot(whole, out_weight[...])
    value = value.astype(BF).astype(F32).reshape(2, 3, 48, D)
    for f in range(4):
        skip[:, pl.ds(3 - start, 3), f] = value[..., 128 * f : 128 * f + 128]
    middle = osum[:, :, mid] * pl.reciprocal(wsum[:, :, mid], approx=True)
    value = dot(middle.reshape(192, D).astype(BF), out_weight[...]).reshape(2, 3, 32, D)
    value = (xj[...].astype(F32)[:, :, mid] + value).astype(BF).astype(F32)
    for f in range(4):
        skip[:, pl.ds(start, 3), f, mid] = value[..., 128 * f : 128 * f + 128]


def last_kernel(
    corners_left, corners_right, xj, qj, edge_sum, edge_weight, most, qkv, gain, out_weight,
    merge_weight, merge_gain, split_weight, split_gain, out, skip, fine, done_rows, sems,
):
    block = head_blocks()
    start = 3 * lax.rem(lax.axis_index("lat"), 2)
    corners = jnp.concatenate([corners_left[...], corners_right[...]], 0)
    k, v = keys_values(corners, qkv, gain[...], block)
    nears = [slice(40 * side, 40 * side + 8) for side in range(2)]
    spots = [(near, lv, r) for near in nears for lv in range(2) for r in range(3)]
    q = jnp.concatenate([qj[lv, r, near] for near, lv, r in spots], 0)
    mask = corner_mask(present_rows())
    attended = []
    for hg in range(2):
        feats = slice(256 * hg, 256 * hg + 256)
        oc, wc = scores_to_sums(q[:, feats], k[:, feats], v[:, feats], mask)
        weight = edge_weight[:, feats] + wc
        attended.append((edge_sum[:, feats] + oc) * pl.reciprocal(weight, approx=True))
    value = dot(jnp.concatenate(attended, 1).astype(BF), out_weight[...])
    own = xj[...].astype(F32)
    skip[...] = most[...]
    for i, (near, lv, r) in enumerate(spots):
        cell = (own[lv, r, near] + value[8 * i : 8 * i + 8]).astype(BF).astype(F32)
        for f in range(4):
            skip[lv, start + r, f, near] = cell[:, 128 * f : 128 * f + 128]
    groups = []
    for c in range(2):
        for r in range(2):
            pieces = []
            for lv in range(2):
                for a in range(3):
                    chunks = [skip[lv, 2 * a + r, f, pl.ds(c, 24, stride=2), :] for f in range(4)]
                    pieces.append(jnp.concatenate(chunks, 1))
            groups.append(jnp.concatenate(pieces, 0))
    mean = sum(jnp.sum(g, -1, keepdims=True) for g in groups) * (1.0 / 2048)
    centered = [g - mean for g in groups]
    variance = sum(jnp.sum(g * g, -1, keepdims=True) for g in centered) * (1.0 / 2048)
    inverse = lax.rsqrt(variance + 1e-05)
    coarse = 0.0
    for i, g in enumerate(centered):
        part = slice(D * i, D * i + D)
        normed = (g * inverse * merge_gain[:, part]).astype(BF)
        coarse = coarse + dot(normed, merge_weight[part])
    coarse = coarse.astype(BF)
    copies = []
    for r in range(2):
        for c in range(2):
            i = 2 * c + r
            expanded = dot(coarse, split_weight[:, D * i : D * i + D])
            done = groups[i] + layer_norm(expanded, split_gain[...])
            for lv in range(2):
                for a in range(3):
                    at = (lv * 3 + a) * 24
                    for f in range(4):
                        fine[lv, 2 * a + r, f, pl.ds(c, 24, stride=2), :] = done[
                            at : at + 24, 128 * f : 128 * f + 128
                        ]
        for lv in range(2):
            for a in range(3):
                row = 2 * a + r
                for f in range(4):
                    done_rows[lv, row, :, 128 * f : 128 * f + 128] = fine[lv, row, f].astype(BF)
                at = (lv, row)
                copies.append(
                    pltpu.make_async_copy(done_rows.at[at], out.at[at], sems.at[lv, row])
                )
                copies[-1].start()
    for copy in copies:
        copy.wait()


def body(
    tokens,
    qkv_weight,
    out_weight,
    attn_gain,
    logit_scale,
    merge_weight,
    merge_gain,
    split_weight,
    split_gain,
):
    lats = lax.axis_size("lat")
    pair = [(i, i ^ 1) for i in range(lats)]
    cross = [(i, ((i + 1) ^ 1) - 1) for i in range(1, lats - 1)]

    def along(value, steps):
        count = lax.axis_size("lon")
        return lax.ppermute(value, "lon", [(i, (i + steps) % count) for i in range(count)])

    def cells(dtype):
        return jax.ShapeDtypeStruct((2, 3, 48, D), dtype)

    xj, xi = pl.pallas_call(
        rows_kernel,
        name="rows",
        out_shape=[cells(BF), cells(BF)],
        in_specs=[VMEM],
        out_specs=[VMEM] * 2,
        compiler_params=PARAMS,
        cost_estimate=pl.CostEstimate(flops=5 * 10**9, bytes_accessed=10**6, transcendentals=0),
    )(tokens)
    ri = lax.ppermute(xi, "lat", pair)
    rj = lax.ppermute(xj, "lat", cross)

    def edge_cells(own):
        near = jnp.concatenate([xi[:, :, own], ri[:, :, own]], 1).reshape(96, D)
        return jnp.concatenate([near, xj[:, :, own].reshape(48, D)], 0)

    first, final = slice(0, 8), slice(40, 48)
    to_left, to_right, ri = lax.optimization_barrier((edge_cells(first), edge_cells(final), ri))
    left = along(to_right, 1)
    right = along(to_left, -1)
    gain = attn_gain.reshape(1, D)

    scales = logit_scale.reshape(1, 8)
    qj, kj, vj = pl.pallas_call(
        own_kernel,
        name="own_far_rows",
        out_shape=[cells(F32)] + [cells(BF)] * 2,
        in_specs=[VMEM] * 4,
        out_specs=[VMEM] * 3,
        compiler_params=PARAMS,
        cost_estimate=pl.CostEstimate(flops=3 * 10**9, bytes_accessed=4 * 10**6, transcendentals=10**6),
    )(xj, qkv_weight, gain, scales)
    qi, ki, vi, kn, vn = pl.pallas_call(
        near_kernel,
        name="near_rows",
        out_shape=[cells(F32)] + [cells(BF)] * 4,
        in_specs=[VMEM] * 5,
        out_specs=[VMEM] * 5,
        compiler_params=PARAMS,
        cost_estimate=pl.CostEstimate(flops=10**7, bytes_accessed=2 * 10**6, transcendentals=10**5),
    )(xi, ri, qkv_weight, gain, scales)
    corner_left, corner_right, rj, qj, kn = lax.optimization_barrier(
        (rj[:, :, first].reshape(48, D), rj[:, :, final].reshape(48, D), rj, qj, kn)
    )
    corners_left = along(corner_right, 1)
    corners_right = along(corner_left, -1)
    flat = jax.ShapeDtypeStruct((96, D), F32)
    chunked = jax.ShapeDtypeStruct((2, 6, 4, 48, 128), F32)
    most, edge_sum, edge_weight = pl.pallas_call(
        far_kernel,
        name="far_rows_and_edges",
        out_shape=[chunked, flat, flat],
        in_specs=[VMEM] * 16,
        out_specs=[VMEM] * 3,
        scratch_shapes=[pltpu.VMEM((2, 3, 48, D), F32)] * 2
        + [pltpu.VMEM((2, 3, 48, D), BF)] * 2
        + [pltpu.VMEM((2, 144, D), BF)] * 2
        + [pltpu.VMEM((2, 3, 48, D), F32)],
        compiler_params=PARAMS,
        cost_estimate=pl.CostEstimate(flops=5 * 10**8, bytes_accessed=4 * 10**6, transcendentals=10**6),
    )(rj, left, right, xj, xi, qkv_weight, gain, out_weight, qj, qi, kj, vj, ki, vi, kn, vn)
    return pl.pallas_call(
        last_kernel,
        name="corners_merge_split",
        out_shape=jax.ShapeDtypeStruct((2, 6, 48, D), BF),
        in_specs=[VMEM] * 14,
        out_specs=pl.BlockSpec(memory_space=pl.ANY),
        scratch_shapes=[
            pltpu.VMEM((2, 6, 4, 48, 128), F32),
            pltpu.VMEM((2, 6, 4, 48, 128), F32),
            pltpu.VMEM((2, 6, 48, D), BF),
            pltpu.SemaphoreType.DMA((2, 6)),
        ],
        compiler_params=PARAMS,
        cost_estimate=pl.CostEstimate(flops=3 * 10**9, bytes_accessed=12 * 10**6, transcendentals=10**6),
    )(
        corners_left, corners_right, xj, qj, edge_sum, edge_weight, most, qkv_weight, gain, out_weight,
        merge_weight, merge_gain.reshape(1, 4 * D), split_weight, split_gain.reshape(1, D),
    )


def solution(mesh):
    placed = (P(None, "lat", "lon", None), P(), P(), P(), P(), P(), P(), P(), P())
    return jax.shard_map(
        body, mesh=mesh, in_specs=placed, out_specs=P(None, "lat", "lon", None), check_vma=False
    )
```
